512 devices in a mesh: dp: 8 (over y_hi, x), mp: 64 (over z, y_lo, core).
Axes of the slice: x: 4, y: 4 (y_hi: 2, y_lo: 2; y = y_hi * 2 + y_lo), z: 16, core: 2. Of those that a mesh axis runs over, the one named last changes fastest.
Arguments:
- activations: bfloat16 [8192, 4096], P(('dp', 'mp')), may hold values from -6 to 6
- out_grads: bfloat16 [8192, 16384], P('dp', 'mp'), may hold values from -0.1875 to 0.1875
- momentum: bfloat16 [8, 4096, 16384], P('dp', None, 'mp'), may hold values from -6 to 6
Outputs:
- remaining: bfloat16 [8, 4096, 16384], P('dp', None, 'mp')
- update: bfloat16 [4096, 16384], P('dp', 'mp')
The draws below stay inside these ranges and needn't reach their ends.
All inputs are finite; a program needn't handle non-finite values.
Results may differ from the reference program's by a relative error of at most 0.001.
Values may be sent and summed in bfloat16 or wider, within the bound.
A program may use at most 64 MiB of HBM per device.

```python
import jax
import jax.numpy as jnp
from jax import lax

D = 4096
FF = 16384
TOKENS = 1024
GROUPS = 8


def levels(own_key, dims, split, least, top_value):
    def one(dim, blocks):
        steps = jax.random.uniform(jax.random.fold_in(jax.random.fold_in(own_key, 6), dim), (blocks,), jnp.float32, least / len(split), top_value / len(split))
        return jnp.repeat(jnp.exp(steps), dims[dim] // blocks).reshape((-1,) + (1,) * (len(dims) - dim - 1))

    level = one(*split[0])
    for cut in split[1:]:
        level = level * one(*cut)
    return level


def normal_values(key, dims, width, reach, pieces=(), held_as=jnp.bfloat16):
    entries = jax.random.normal(key, dims, jnp.float32) * width
    if len(pieces) > 0:
        entries = levels(key, dims, pieces, -0.22, 0.18) * entries
    return jnp.clip(entries, min=-reach, max=reach).astype(held_as)


def setup_inputs(seed: int = 0) -> dict:
    seeds = jax.random.split(jax.random.key(seed), 4)
    return {
        "activations": normal_values(seeds[0], (GROUPS * TOKENS, D), 1.0, 6.0, ((0, 512),)),
        "out_grads": normal_values(seeds[1], (GROUPS * TOKENS, FF), (TOKENS ** -0.5), 0.1875, ((0, 8), (1, 64))),
        "momentum": normal_values(seeds[2], (GROUPS, D, FF), 1.0, 6.0, ((0, 8), (2, 64))),
    }


BETA = 0.9
EPSILON = 1e-06

def low_basis():
    order = jnp.arange(8, dtype=jnp.float32)[:, None]
    position = jnp.arange(64, dtype=jnp.float32)[None, :]
    factor = jnp.where(order == 0, 0.125, 0.17677669529663687).astype(jnp.float32)
    return (factor * jnp.cos(jnp.pi * (2.0 * position + 1.0) * order / 128.0)).astype(jnp.float32)

def forward_low(matrix_in, dct_basis):
    row_count, col_count = matrix_in.shape
    left_part = jnp.einsum('ar,prf->paf', dct_basis, matrix_in.reshape(row_count // 64, 64, col_count), precision=lax.Precision.HIGHEST)
    return jnp.einsum('paqs,bs->paqb', left_part.reshape(row_count // 64, 8, col_count // 64, 64), dct_basis, precision=lax.Precision.HIGHEST)

def inverse_low(low_block, dct_basis):
    band_count, _, span_count, _ = low_block.shape
    right_part = jnp.einsum('paqb,bs->paqs', low_block, dct_basis, precision=lax.Precision.HIGHEST).reshape(band_count, 8, span_count * 64)
    return jnp.einsum('ar,paf->prf', dct_basis, right_part, precision=lax.Precision.HIGHEST).reshape(band_count * 64, span_count * 64)

def soft_sign(matrix_in):
    row_count, col_count = matrix_in.shape
    spans = matrix_in.reshape(row_count // 64, 64, col_count // 64, 64)
    span_power = lax.optimization_barrier(jnp.mean(spans * spans, axis=(1, 3), keepdims=True))
    return jnp.tanh(spans / jnp.sqrt(span_power + EPSILON)).reshape(row_count, col_count)

def reference(activations, out_grads, momentum):
    dct_basis = low_basis()

    def one_group(group_index):
        first_row = (group_index * TOKENS).astype(jnp.int32)
        group_acts = lax.dynamic_slice_in_dim(activations, first_row, TOKENS, 0)
        group_grads = lax.dynamic_slice_in_dim(out_grads, first_row, TOKENS, 0)
        gradient = lax.dot_general(group_acts, group_grads, (((0,), (0,)), ((), ())), preferred_element_type=jnp.float32)
        old_state = lax.dynamic_index_in_dim(momentum, group_index, 0, keepdims=False).astype(jnp.float32)
        moved = BETA * old_state + gradient
        low_block = forward_low(moved, dct_basis)
        remaining = (moved - inverse_low(low_block, dct_basis)).astype(jnp.bfloat16)
        return (remaining, low_block)
    remaining, blocks = lax.map(one_group, jnp.arange(GROUPS, dtype=jnp.int32))
    average = lax.optimization_barrier(jnp.sum(blocks, axis=0)) / GROUPS
    update = soft_sign(inverse_low(average, dct_basis)).astype(jnp.bfloat16)
    return (remaining, update)
```

```python
import functools

import jax
import jax.numpy as jnp
import ml_dtypes
import numpy as np
from jax import lax
from jax.experimental import pallas as pl
from jax.experimental.pallas import tpu as pltpu
from jax.sharding import PartitionSpec as P

BETA = 0.9
EPSILON = 1e-06
MESH = pl.DeviceIdType.MESH
NZ = 16
NB = 5
UP, DOWN = 0, 1
F32, BF16 = jnp.float32, jnp.bfloat16


def low_basis():
    order = np.arange(8)[:, None]
    position = np.arange(64)[None, :]
    factor = np.where(order == 0, 0.125, np.sqrt(2.0 / 64.0))
    return (factor * np.cos(np.pi * (2 * position + 1) * order / 128.0)).astype(np.float32)


def pieces_np(x):
    one = x.astype(ml_dtypes.bfloat16)
    rest = x - one.astype(np.float32)
    two = rest.astype(ml_dtypes.bfloat16)
    three = (rest - two.astype(np.float32)).astype(ml_dtypes.bfloat16)
    return one, two, three


def constants():
    b = low_basis()
    kb = np.kron(np.eye(4, dtype=np.float32), b)
    k1, k2, k3 = pieces_np(kb)
    zero = np.zeros_like(k1)
    first = np.concatenate([np.eye(256, dtype=ml_dtypes.bfloat16), k1, k2, k3], 0)
    wide = [np.tile(k.T, (1, 4)) for k in (k1, k1, k1, k2, k2, k3)]
    to_low = np.concatenate(wide, 0)
    from_low = np.concatenate([k1, k1, k1, k2, k2, k3, zero, zero], 0)
    columns = np.concatenate([k.T for k in (k1, k1, k1, k2, k2, k3)], 1)
    tall = np.concatenate([np.tile(k, (4, 1)) for k in (k1, k1, k1, k2, k2, k3)], 0)
    eight = np.tile(b.T, (4, 1))
    ones = np.kron(np.eye(16, dtype=np.float32), np.ones((8, 8), np.float32)).astype(ml_dtypes.bfloat16)
    return first, to_low, from_low, columns, tall, eight, ones


def pieces(x):
    one = x.astype(BF16)
    rest = x - one.astype(F32)
    two = rest.astype(BF16)
    three = (rest - two.astype(F32)).astype(BF16)
    return one, two, three


def dot(a, b):
    return lax.dot_general(a, b, (((1,), (0,)), ((), ())), preferred_element_type=F32)


def dot_nt(a, b):
    return lax.dot_general(a, b, (((1,), (1,)), ((), ())), preferred_element_type=F32)


def kernel(
    act, grads, mom, c_first, c_to_low, c_from_low, c_columns, c_tall, c_eight, c_ones,
    rem_out, upd_out,
    buf, acc, acc_low, g_in, g_t, m_in, rem, upd, low_out, low_in,
    first, to_low, from_low, columns, tall, eight, ones,
    zr, yr, cr, lr, zs, ys, cs, ls, local, out_sem,
):
    group, lane_id = lax.axis_index("dp"), lax.axis_index("mp")
    z, y, core = lane_id // 4, (lane_id // 2) % 2, lane_id % 2

    def at(zz, yy, cc):
        return {"mp": (zz * 2 + yy) * 2 + cc}

    hop = (at((z + 1) % NZ, y, core), at((z + NZ - 1) % NZ, y, core))
    pair, twin = at(z, 1 - y, core), at(z, y, 1 - core)

    tiles = {"B": (0, NB), "A": (NB, 8 - NB)}
    last = {("B", UP): 8, ("B", DOWN): 7, ("A", UP): 7, ("A", DOWN): 8}
    tall_rows = {"B": 16, "A": 32}
    OWN = 960

    def number(h, kind):
        return h * 2 + (0 if kind == "B" else 1)

    def level(direction, s):
        if isinstance(s, int) and s == 8:
            return 896, 14
        row = (s - 1) * 128 + (64 if direction == DOWN else 0)
        return (row if isinstance(row, int) else pl.multiple_of(row, 64)), (s - 1) * 2 + direction

    def part(h, kind, row, rows):
        begin, count = tiles[kind]
        return buf.at[h, pl.ds(begin, count), pl.ds(row, rows)]

    def remote(src, dst, send, recv, device):
        return pltpu.make_async_remote_copy(
            src_ref=src, dst_ref=dst, send_sem=send, recv_sem=recv, device_id=device, device_id_type=MESH
        )

    def z_copy(h, kind, direction, s):
        n, rows = number(h, kind), tall_rows[kind]
        src = OWN if isinstance(s, int) and s == 1 else level(direction, s - 1)[0]
        dst, _ = level(direction, s)
        return remote(
            part(h, kind, src, rows), part(h, kind, dst, rows),
            zs.at[direction, n], zr.at[direction, n, s - 1], hop[direction],
        )

    def y_copy(h, kind, row, index):
        n = number(h, kind)
        return remote(
            part(h, kind, row, 16), part(h, kind, row + 16, 16), ys.at[n], yr.at[n, index], pair
        )

    def c_copy(h, kind, row, index):
        n = number(h, kind)
        return remote(
            part(h, kind, row, 32), part(h, kind, row + 32, 32), cs.at[n], cr.at[n, index], twin
        )

    def directions(kind, s):
        if not isinstance(s, int):
            return (UP, DOWN)
        return tuple(d for d in (UP, DOWN) if 1 <= s <= last[kind, d])

    def on_z(h, kind, s):
        for direction in directions(kind, s):
            z_copy(h, kind, direction, s).wait_recv()
            if not isinstance(s, int) or s < last[kind, direction]:
                z_copy(h, kind, direction, s + 1).start()
            row, index = level(direction, s)
            (y_copy if kind == "B" else c_copy)(h, kind, row, index).start()

    def on_y(h, s):
        for direction in directions("B", s):
            row, index = level(direction, s)
            y_copy(h, "B", row, index).wait_recv()
            c_copy(h, "B", row, index).start()

    def add_product(h, kind, s):
        for direction in directions(kind, s):
            row, index = level(direction, s)
            c_copy(h, kind, row, index).wait_recv()
        if isinstance(s, int) and s == 8:
            c_copy(h, kind, OWN, 15).wait_recv()
        begin, count = tiles[kind]
        rows = (s - 1) * 128
        rows = rows if isinstance(rows, int) else pl.multiple_of(rows, 128)
        left = g_t[s - 1]

        @pl.loop(begin, begin + count)
        def _(d):
            product = dot(left, buf[h, d, pl.ds(rows, 128), :])
            acc[h, d] += product[:256]
            acc_low[h, d] += product[256:288] + product[288:320] + product[320:352]

    def start_sum(h, kind):
        begin, count = tiles[kind]

        @pl.loop(begin, begin + count)
        def _(d):
            rows = pl.multiple_of(d * 512 + h * 256, 256)
            product = dot_nt(first[...], m_in[pl.ds(rows, 256), :])
            acc[h, d] = BETA * product[:256]
            acc_low[h, d] = BETA * (product[256:288] + product[288:320] + product[320:352])

    lane_group = lax.broadcasted_iota(jnp.int32, (8, 128), 1) // 32

    def by_lanes(a, b, c, d):
        g = lax.broadcasted_iota(jnp.int32, a.shape, 1) // 32
        return jnp.where(g == 0, a, jnp.where(g == 1, b, jnp.where(g == 2, c, d)))

    low_keep = {}

    def low_of(h, kind):
        begin, count = tiles[kind]
        x = acc_low[h, begin : begin + count].reshape(count * 32, 256)
        x1, x2, x3 = pieces(x)
        low = dot(jnp.concatenate([x1, x2, x3, x1, x2, x1], 1), to_low[...])
        low_keep[h, kind] = low
        for i in range(count):
            d = begin + i
            block = [low[i * 32 + 8 * k : i * 32 + 8 * k + 8] for k in range(4)]
            low_out[h, d] = by_lanes(*block)
        for i in range(count):
            d = begin + i
            slot = (group - d + 8) % 8

            @pl.when(d != group)
            def _(d=d, slot=slot):
                remote(low_out.at[h, d], low_in.at[h, slot], ls.at[h], lr.at[h, slot], {"dp": d}).start()

    def remaining_of(h, kind):
        begin, count = tiles[kind]
        l1, l2, l3 = pieces(low_keep[h, kind])
        zero = jnp.zeros_like(l1)
        left = jnp.concatenate([by_lanes(l1, l2, l3, l1), by_lanes(l2, l1, zero, zero)], 1)
        w = dot(left, from_low[...])
        for i in range(count):
            d = begin + i
            w1, w2, w3 = pieces(w[i * 32 : i * 32 + 32])
            expanded = dot(columns[...], jnp.concatenate([w1, w2, w3, w1, w2, w1], 0))
            rest = (acc[h, d] - expanded).T.astype(BF16)
            row = d * 512 + h * 256
            rem[row : row + 256, :] = rest
            pltpu.make_async_copy(
                rem.at[pl.ds(row, 256)], rem_out.at[pl.ds(row, 256)], out_sem.at[0]
            ).start()

    def update_of(h):
        for k in range(1, 8):
            remote(low_out.at[h, 0], low_in.at[h, k], ls.at[h], lr.at[h, k], {"dp": group}).wait_recv()
        total = low_out[h, group]
        for k in range(1, 8):
            total = total + low_in[h, k]
        average = total * 0.125
        square = jnp.sum(average * average, axis=0, keepdims=True)
        s1, s2, s3 = pieces(jnp.broadcast_to(square, (8, 128)))
        power = (dot(s1, ones[...]) + dot(s2, ones[...]) + dot(s3, ones[...])) * (1.0 / 4096.0)
        scaled = average / jnp.sqrt(power + EPSILON)
        spread = jnp.dot(eight[...], scaled, precision=lax.Precision.HIGHEST, preferred_element_type=F32)
        row_group = lax.broadcasted_iota(jnp.int32, (256, 128), 0) // 64
        lanes = lax.broadcasted_iota(jnp.int32, (256, 128), 1) // 32
        spread = jnp.where(row_group == lanes, spread, 0.0)
        s1, s2, s3 = pieces(spread)
        shared = dot(jnp.concatenate([s1, s2, s3, s1, s2, s1], 1), tall[...])
        upd[h * 256 : h * 256 + 256, :] = jnp.tanh(shared).T.astype(BF16)
        pltpu.make_async_copy(
            upd.at[pl.ds(h * 256, 256)], upd_out.at[pl.ds(h * 256, 256)], out_sem.at[1]
        ).start()

    for h in range(2):
        for d in range(8):
            pltpu.make_async_copy(
                act.at[:, pl.ds(d * 512 + h * 256, 256)], buf.at[h, d, pl.ds(OWN, 16)], local.at[0]
            ).start()

    def own_rows(zz, yo, co):
        m = (zz * 2 + (y + yo) % 2) * 2 + (core + co) % 2
        return pl.multiple_of(m * 16, 16)

    for co in range(2):
        for yo in range(2):
            pltpu.make_async_copy(
                grads.at[pl.ds(own_rows(z, yo, co), 16)], g_in.at[pl.ds(OWN + co * 32 + yo * 16, 16)], local.at[1]
            ).start()

            @pl.loop(0, 15)
            def _(k, co=co, yo=yo):
                s = k // 2 + 1
                zz = (z + NZ - s + (k % 2) * 2 * s) % NZ
                row = pl.multiple_of(k * 64 + co * 32 + yo * 16, 16)
                pltpu.make_async_copy(
                    grads.at[pl.ds(own_rows(zz, yo, co), 16)], g_in.at[pl.ds(row, 16)], local.at[1]
                ).start()

    constant = (
        (c_first, first), (c_to_low, to_low), (c_from_low, from_low), (c_columns, columns),
        (c_tall, tall), (c_eight, eight), (c_ones, ones),
    )
    const_copies = [
        pltpu.make_async_copy(src, dst, local.at[3 + i]) for i, (src, dst) in enumerate(constant)
    ]
    for copy in const_copies:
        copy.start()
    pltpu.make_async_copy(mom, m_in, local.at[2]).start()

    barrier = pltpu.get_barrier_semaphore()
    for device in (*hop, pair, twin):
        pl.semaphore_signal(barrier, inc=1, device_id=device, device_id_type=MESH)
    for k in range(1, 8):
        pl.semaphore_signal(barrier, inc=1, device_id={"dp": (group + k) % 8}, device_id_type=MESH)
    pl.semaphore_wait(barrier, 11)

    own_all = buf.at[:, :, pl.ds(OWN, 16)]
    pltpu.make_async_copy(own_all, own_all, local.at[0]).wait()

    y_copy(0, "A", OWN, 15).start()
    y_copy(1, "A", OWN, 15).start()
    for h in range(2):
        for direction in (UP, DOWN):
            z_copy(h, "B", direction, 1).start()
    y_copy(0, "B", OWN, 15).start()
    y_copy(1, "B", OWN, 15).start()

    const_copies[0].wait()
    pltpu.make_async_copy(g_in, g_in, local.at[1]).wait()

    @pl.loop(0, 8)
    def _(s):
        turned = dot_nt(first[...], g_in[pl.ds(pl.multiple_of(s * 128, 128), 128), :])
        g_t[s, :256] = turned[:256].astype(BF16)
        for i, piece in enumerate(pieces(turned[256:288] + turned[288:320] + turned[320:352])):
            g_t[s, 256 + 32 * i : 288 + 32 * i] = piece

    def both_columns(h):
        y_copy(h, "A", OWN, 15).wait_recv()
        for direction in (UP, DOWN):
            z_copy(h, "A", direction, 1).start()
        c_copy(h, "A", OWN, 15).start()

    def own_column(h):
        y_copy(h, "B", OWN, 15).wait_recv()
        c_copy(h, "B", OWN, 15).start()

    both_columns(0)
    pltpu.make_async_copy(m_in, m_in, local.at[2]).wait()
    start_sum(0, "B")
    on_z(0, "B", 1)
    both_columns(1)
    own_column(0)
    own_column(1)
    start_sum(0, "A")
    on_z(1, "B", 1)
    start_sum(1, "B")
    on_z(0, "A", 1)
    on_y(0, 1)
    add_product(0, "A", 1)
    on_z(0, "B", 2)
    start_sum(1, "A")
    on_y(1, 1)
    add_product(0, "B", 1)

    def step(t):
        static = isinstance(t, int)

        def ok(s):
            return not static or 1 <= s <= 8

        on_z(1, "B", t - 1)
        if ok(t - 3):
            add_product(1, "A", t - 3)
        on_z(0, "A", t - 1)
        add_product(1, "B", t - 2)
        on_z(1, "A", t - 2)
        on_y(0, t - 1)
        add_product(0, "A", t - 1)
        if ok(t):
            on_z(0, "B", t)
        on_y(1, t - 1)
        add_product(0, "B", t - 1)

    step(3)

    @pl.loop(4, 7)
    def _(t):
        step(t)

    step(7)
    step(8)
    for copy in const_copies[1:]:
        copy.wait()
    on_z(1, "B", 8)
    add_product(1, "A", 6)
    on_z(0, "A", 8)
    add_product(1, "B", 7)
    on_z(1, "A", 7)
    on_y(0, 8)
    add_product(0, "A", 8)
    low_of(0, "A")
    on_y(1, 8)
    add_product(0, "B", 8)
    low_of(0, "B")
    add_product(1, "A", 7)
    on_z(1, "A", 8)
    remaining_of(0, "A")
    add_product(1, "B", 8)
    low_of(1, "B")
    add_product(1, "A", 8)
    low_of(1, "A")
    remaining_of(0, "B")
    update_of(0)
    remaining_of(1, "B")
    remaining_of(1, "A")
    update_of(1)

    for h in range(2):
        for kind in ("B", "A"):
            n, rows = number(h, kind), tall_rows[kind]
            for direction in (UP, DOWN):
                sent = part(h, kind, 0, rows * last[kind, direction])
                remote(sent, sent, zs.at[direction, n], zr.at[direction, n, 0], hop[direction]).wait_send()
            sent = part(h, kind, 0, 256 if kind == "B" else 16)
            remote(sent, sent, ys.at[n], yr.at[n, 0], pair).wait_send()
            sent = part(h, kind, 0, 512)
            remote(sent, sent, cs.at[n], cr.at[n, 0], twin).wait_send()
        sent = low_out.at[h, pl.ds(0, 7)]
        remote(sent, sent, ls.at[h], lr.at[h, 0], {"dp": group}).wait_send()
    pltpu.make_async_copy(rem, rem_out, out_sem.at[0]).wait()
    pltpu.make_async_copy(upd, upd_out, out_sem.at[1]).wait()


def body(activations, out_grads, momentum):
    consts = [jnp.asarray(c) for c in constants()]
    any_space = pl.BlockSpec(memory_space=pl.ANY)
    dma = pltpu.SemaphoreType.DMA
    remaining, update = pl.pallas_call(
        kernel,
        name="gather_product_low",
        out_shape=(jax.ShapeDtypeStruct((4096, 256), BF16), jax.ShapeDtypeStruct((512, 256), BF16)),
        in_specs=[any_space] * 10,
        out_specs=(any_space, any_space),
        scratch_shapes=[
            pltpu.VMEM((2, 8, 1024, 256), BF16),
            pltpu.VMEM((2, 8, 256, 256), F32),
            pltpu.VMEM((2, 8, 32, 256), F32),
            pltpu.VMEM((1024, 256), BF16),
            pltpu.VMEM((8, 352, 128), BF16),
            pltpu.VMEM((4096, 256), BF16),
            pltpu.VMEM((4096, 256), BF16),
            pltpu.VMEM((512, 256), BF16),
            pltpu.VMEM((2, 8, 8, 128), F32),
            pltpu.VMEM((2, 8, 8, 128), F32),
            *[pltpu.VMEM(c.shape, c.dtype) for c in consts],
            dma((2, 4, 8)),
            dma((4, 16)),
            dma((4, 16)),
            dma((2, 8)),
            dma((2, 4)),
            dma((4,)),
            dma((4,)),
            dma((2,)),
            dma((10,)),
            dma((2,)),
        ],
        compiler_params=pltpu.CompilerParams(
            collective_id=0, has_side_effects=True, vmem_limit_bytes=48 * 1024 * 1024
        ),
        cost_estimate=pl.CostEstimate(flops=2 * 1024 * 4096 * 352, bytes_accessed=5 << 20, transcendentals=512 * 256),
    )(activations, out_grads, momentum[0], *consts)
    return remaining[None], update


def solution(mesh):
    return jax.shard_map(
        body,
        mesh=mesh,
        in_specs=(P(("dp", "mp"), None), P("dp", "mp"), P("dp", None, "mp")),
        out_specs=(P("dp", None, "mp"), P("dp", "mp")),
        check_vma=False,
    )
```

```python
import functools

import jax
import jax.numpy as jnp
import ml_dtypes
import numpy as np
from jax import lax
from jax.experimental import pallas as pl
from jax.experimental.pallas import tpu as pltpu
from jax.sharding import PartitionSpec as P

BETA = 0.9
EPSILON = 1e-06
MESH = pl.DeviceIdType.MESH
NZ = 16
NB = 5
UP, DOWN = 0, 1
F32, BF16 = jnp.float32, jnp.bfloat16


def low_basis():
    order = np.arange(8)[:, None]
    position = np.arange(64)[None, :]
    factor = np.where(order == 0, 0.125, np.sqrt(2.0 / 64.0))
    return (factor * np.cos(np.pi * (2 * position + 1) * order / 128.0)).astype(np.float32)


def pieces_np(x):
    one = x.astype(ml_dtypes.bfloat16)
    rest = x - one.astype(np.float32)
    two = rest.astype(ml_dtypes.bfloat16)
    three = (rest - two.astype(np.float32)).astype(ml_dtypes.bfloat16)
    return one, two, three


def constants():
    b = low_basis()
    kb = np.kron(np.eye(4, dtype=np.float32), b)
    k1, k2, k3 = pieces_np(kb)
    zero = np.zeros_like(k1)
    first = np.concatenate([k1, k2, k3], 0)
    wide = [np.tile(k.T, (1, 4)) for k in (k1, k1, k1, k2, k2, k3)]
    to_low = np.concatenate(wide, 0)
    from_low = np.concatenate([k1, k1, k1, k2, k2, k3, zero, zero], 0)
    columns = np.concatenate([k.T for k in (k1, k1, k1, k2, k2, k3)], 1)
    tall = np.concatenate([np.tile(k, (4, 1)) for k in (k1, k1, k1, k2, k2, k3)], 0)
    eight = np.tile(b.T, (4, 1))
    ones = np.kron(np.eye(16, dtype=np.float32), np.ones((8, 8), np.float32)).astype(ml_dtypes.bfloat16)
    return first, to_low, from_low, columns, tall, eight, ones


def pieces(x):
    one = x.astype(BF16)
    rest = x - one.astype(F32)
    two = rest.astype(BF16)
    three = (rest - two.astype(F32)).astype(BF16)
    return one, two, three


def dot(a, b):
    return lax.dot_general(a, b, (((1,), (0,)), ((), ())), preferred_element_type=F32)


def kernel(
    act, grads, mom, c_first, c_to_low, c_from_low, c_columns, c_tall, c_eight, c_ones,
    rem, upd,
    buf, acc, acc_low, g_in, g_t, m_in, low_out, low_in,
    first, to_low, from_low, columns, tall, eight, ones,
    zr, yr, cr, lr, zs, ys, cs, ls, local,
):
    group, lane_id = lax.axis_index("dp"), lax.axis_index("mp")
    z, y, core = lane_id // 4, (lane_id // 2) % 2, lane_id % 2

    def at(zz, yy, cc):
        return {"mp": (zz * 2 + yy) * 2 + cc}

    hop = (at((z + 1) % NZ, y, core), at((z + NZ - 1) % NZ, y, core))
    pair, twin = at(z, 1 - y, core), at(z, y, 1 - core)

    tiles = {"B": (0, NB), "A": (NB, 8 - NB)}
    last = {("B", UP): 8, ("B", DOWN): 7, ("A", UP): 7, ("A", DOWN): 8}
    tall_rows = {"B": 16, "A": 32}
    OWN = 960

    def number(h, kind):
        return h * 2 + (0 if kind == "B" else 1)

    def level(direction, s):
        if isinstance(s, int) and s == 8:
            return 896, 14
        row = (s - 1) * 128 + (64 if direction == DOWN else 0)
        return (row if isinstance(row, int) else pl.multiple_of(row, 64)), (s - 1) * 2 + direction

    def part(h, kind, row, rows):
        begin, count = tiles[kind]
        return buf.at[h, pl.ds(begin, count), pl.ds(row, rows)]

    def remote(src, dst, send, recv, device):
        return pltpu.make_async_remote_copy(
            src_ref=src, dst_ref=dst, send_sem=send, recv_sem=recv, device_id=device, device_id_type=MESH
        )

    def z_copy(h, kind, direction, s):
        n, rows = number(h, kind), tall_rows[kind]
        src = OWN if isinstance(s, int) and s == 1 else level(direction, s - 1)[0]
        dst, _ = level(direction, s)
        return remote(
            part(h, kind, src, rows), part(h, kind, dst, rows),
            zs.at[direction, n], zr.at[direction, n, s - 1], hop[direction],
        )

    def y_copy(h, kind, row, index):
        n = number(h, kind)
        return remote(
            part(h, kind, row, 16), part(h, kind, row + 16, 16), ys.at[n], yr.at[n, index], pair
        )

    def c_copy(h, kind, row, index):
        n = number(h, kind)
        return remote(
            part(h, kind, row, 32), part(h, kind, row + 32, 32), cs.at[n], cr.at[n, index], twin
        )

    def directions(kind, s):
        if not isinstance(s, int):
            return (UP, DOWN)
        return tuple(d for d in (UP, DOWN) if 1 <= s <= last[kind, d])

    def on_z(h, kind, s):
        for direction in directions(kind, s):
            z_copy(h, kind, direction, s).wait_recv()
            if not isinstance(s, int) or s < last[kind, direction]:
                z_copy(h, kind, direction, s + 1).start()
            row, index = level(direction, s)
            (y_copy if kind == "B" else c_copy)(h, kind, row, index).start()

    def on_y(h, kind, s):
        for direction in directions(kind, s):
            row, index = level(direction, s)
            y_copy(h, kind, row, index).wait_recv()
            c_copy(h, kind, row, index).start()

    def add_product(h, kind, s):
        for direction in directions(kind, s):
            row, index = level(direction, s)
            c_copy(h, kind, row, index).wait_recv()
        if isinstance(s, int) and s == 8:
            c_copy(h, kind, OWN, 15).wait_recv()
        begin, count = tiles[kind]
        rows = (s - 1) * 128
        rows = rows if isinstance(rows, int) else pl.multiple_of(rows, 128)
        left = g_t[s - 1]

        for d in range(begin, begin + count):
            product = dot(left, buf[h, d, pl.ds(rows, 128), :])
            acc[h, d] += product[:256]
            acc_low[h, d] += product[256:288] + product[288:320] + product[320:352]

    def start_sum(h, kind):
        begin, count = tiles[kind]

        for d in range(begin, begin + count):
            row = d * 512 + h * 256
            turned = m_in[row : row + 256, :].T
            acc[h, d] = BETA * turned.astype(F32)
            product = dot(first[...], turned)
            acc_low[h, d] = BETA * (product[:32] + product[32:64] + product[64:])

    def by_lanes(a, b, c, d):
        g = lax.broadcasted_iota(jnp.int32, a.shape, 1) // 32
        return jnp.where(g == 0, a, jnp.where(g == 1, b, jnp.where(g == 2, c, d)))

    low_keep = {}

    def low_of(h, kind):
        begin, count = tiles[kind]
        x = acc_low[h, begin : begin + count].reshape(count * 32, 256)
        x1, x2, x3 = pieces(x)
        low = dot(jnp.concatenate([x1, x2, x3, x1, x2, x1], 1), to_low[...])
        low_keep[h, kind] = low
        for i in range(count):
            d = begin + i
            block = [low[i * 32 + 8 * k : i * 32 + 8 * k + 8] for k in range(4)]
            low_out[h, d] = by_lanes(*block)
        for i in range(count):
            d = begin + i
            slot = (group - d + 8) % 8

            @pl.when(d != group)
            def _(d=d, slot=slot):
                remote(low_out.at[h, d], low_in.at[h, slot], ls.at[h], lr.at[h, slot], {"dp": d}).start()

    def remaining_of(h, kind):
        begin, count = tiles[kind]
        l1, l2, l3 = pieces(low_keep[h, kind])
        zero = jnp.zeros_like(l1)
        left = jnp.concatenate([by_lanes(l1, l2, l3, l1), by_lanes(l2, l1, zero, zero)], 1)
        w = dot(left, from_low[...])
        for i in range(count):
            d = begin + i
            w1, w2, w3 = pieces(w[i * 32 : i * 32 + 32])
            expanded = dot(columns[...], jnp.concatenate([w1, w2, w3, w1, w2, w1], 0))
            rest = (acc[h, d] - expanded).T.astype(BF16)
            row = d * 512 + h * 256
            rem[row : row + 256, :] = rest

    def update_of(h):
        for k in range(1, 8):
            remote(low_out.at[h, 0], low_in.at[h, k], ls.at[h], lr.at[h, k], {"dp": group}).wait_recv()
        total = low_out[h, group]
        for k in range(1, 8):
            total = total + low_in[h, k]
        average = total * 0.125
        square = jnp.sum(average * average, axis=0, keepdims=True)
        s1, s2, s3 = pieces(jnp.broadcast_to(square, (8, 128)))
        power = (dot(s1, ones[...]) + dot(s2, ones[...]) + dot(s3, ones[...])) * (1.0 / 4096.0)
        scaled = average / jnp.sqrt(power + EPSILON)
        spread = jnp.dot(eight[...], scaled, precision=lax.Precision.HIGHEST, preferred_element_type=F32)
        row_group = lax.broadcasted_iota(jnp.int32, (256, 128), 0) // 64
        lanes = lax.broadcasted_iota(jnp.int32, (256, 128), 1) // 32
        spread = jnp.where(row_group == lanes, spread, 0.0)
        s1, s2, s3 = pieces(spread)
        shared = dot(jnp.concatenate([s1, s2, s3, s1, s2, s1], 1), tall[...])
        upd[h * 256 : h * 256 + 256, :] = jnp.tanh(shared).T.astype(BF16)

    barrier = pltpu.get_barrier_semaphore()
    for device in (*hop, pair, twin):
        pl.semaphore_signal(barrier, inc=1, device_id=device, device_id_type=MESH)
    for k in range(1, 8):
        pl.semaphore_signal(barrier, inc=1, device_id={"dp": (group + k) % 8}, device_id_type=MESH)

    for h in range(2):
        for d in range(8):
            pltpu.make_async_copy(
                act.at[:, pl.ds(d * 512 + h * 256, 256)], buf.at[h, d, pl.ds(OWN, 16)], local.at[0]
            ).start()

    def own_rows(zz, yo, co):
        m = (zz * 2 + (y + yo) % 2) * 2 + (core + co) % 2
        return pl.multiple_of(m * 16, 16)

    for co in range(2):
        for yo in range(2):
            pltpu.make_async_copy(
                grads.at[pl.ds(own_rows(z, yo, co), 16)], g_in.at[pl.ds(OWN + co * 32 + yo * 16, 16)], local.at[1]
            ).start()

            @pl.loop(0, 15)
            def _(k, co=co, yo=yo):
                s = k // 2 + 1
                zz = (z + NZ - s + (k % 2) * 2 * s) % NZ
                row = pl.multiple_of(k * 64 + co * 32 + yo * 16, 16)
                pltpu.make_async_copy(
                    grads.at[pl.ds(own_rows(zz, yo, co), 16)], g_in.at[pl.ds(row, 16)], local.at[1]
                ).start()

    constant = (
        (c_first, first), (c_to_low, to_low), (c_from_low, from_low), (c_columns, columns),
        (c_tall, tall), (c_eight, eight), (c_ones, ones),
    )
    const_copies = [
        pltpu.make_async_copy(src, dst, local.at[3 + i]) for i, (src, dst) in enumerate(constant)
    ]
    for copy in const_copies:
        copy.start()
    pltpu.make_async_copy(mom, m_in, local.at[2]).start()

    pl.semaphore_wait(barrier, 11)

    own_all = buf.at[:, :, pl.ds(OWN, 16)]
    pltpu.make_async_copy(own_all, own_all, local.at[0]).wait()

    y_copy(0, "A", OWN, 15).start()
    y_copy(1, "A", OWN, 15).start()
    for h in range(2):
        for direction in (UP, DOWN):
            z_copy(h, "B", direction, 1).start()
    y_copy(0, "B", OWN, 15).start()
    y_copy(1, "B", OWN, 15).start()

    const_copies[0].wait()
    pltpu.make_async_copy(g_in, g_in, local.at[1]).wait()

    for s in range(8):
        turned = g_in[s * 128 : s * 128 + 128, :].T
        g_t[s, :256] = turned
        product = dot(first[...], turned)
        for i, piece in enumerate(pieces(product[:32] + product[32:64] + product[64:])):
            g_t[s, 256 + 32 * i : 288 + 32 * i] = piece

    def both_columns(h):
        y_copy(h, "A", OWN, 15).wait_recv()
        for direction in (UP, DOWN):
            z_copy(h, "A", direction, 1).start()
        c_copy(h, "A", OWN, 15).start()

    def own_column(h):
        y_copy(h, "B", OWN, 15).wait_recv()
        c_copy(h, "B", OWN, 15).start()

    slot = (
        (on_z, 1, "A", 2), (add_product, 1, "A", 3), (on_z, 0, "B", 0), (on_y, 0, "B", 1), (add_product, 1, "B", 2),
        (add_product, 0, "A", 1), (on_z, 1, "B", 0), (on_z, 0, "A", 0), (on_y, 1, "B", 1), (add_product, 0, "B", 1),
    )

    def run_slot(t):
        for task, h, kind, lag in slot:
            if not isinstance(t, int) or 1 <= t - lag <= 8:
                task(h, kind, t - lag)
                if task is add_product and isinstance(t, int) and t - lag == 8:
                    low_of(h, kind)

    both_columns(0)
    run_slot(1)
    both_columns(1)
    pltpu.make_async_copy(m_in, m_in, local.at[2]).wait()
    start_sum(0, "A")
    start_sum(0, "B")
    run_slot(2)
    own_column(0)
    own_column(1)
    start_sum(1, "B")
    start_sum(1, "A")
    run_slot(3)

    @pl.loop(4, 7)
    def _(t):
        run_slot(t)

    run_slot(7)
    run_slot(8)
    for copy in const_copies[1:]:
        copy.wait()
    run_slot(9)
    run_slot(10)
    run_slot(11)
    remaining_of(0, "A")
    remaining_of(0, "B")
    update_of(0)
    remaining_of(1, "B")
    remaining_of(1, "A")
    update_of(1)

    for h in range(2):
        for kind in ("B", "A"):
            n, rows = number(h, kind), tall_rows[kind]
            for direction in (UP, DOWN):
                sent = part(h, kind, 0, rows * last[kind, direction])
                remote(sent, sent, zs.at[direction, n], zr.at[direction, n, 0], hop[direction]).wait_send()
            sent = part(h, kind, 0, 256 if kind == "B" else 16)
            remote(sent, sent, ys.at[n], yr.at[n, 0], pair).wait_send()
            sent = part(h, kind, 0, 512)
            remote(sent, sent, cs.at[n], cr.at[n, 0], twin).wait_send()
        sent = low_out.at[h, pl.ds(0, 7)]
        remote(sent, sent, ls.at[h], lr.at[h, 0], {"dp": group}).wait_send()


def store_kernel(rem, upd, rem_out, upd_out, sem):
    copies = [pltpu.make_async_copy(upd, upd_out, sem.at[0])]
    for i in range(4):
        rows = pl.ds(i * 1024, 1024)
        copies.append(pltpu.make_async_copy(rem.at[rows], rem_out.at[rows], sem.at[1 + i]))
    for copy in copies:
        copy.start()
    for copy in copies:
        copy.wait()


def body(activations, out_grads, momentum):
    consts = [jnp.asarray(c) for c in constants()]
    shapes = ((4096, 256), (512, 256))
    any_space = pl.BlockSpec(memory_space=pl.ANY)
    dma = pltpu.SemaphoreType.DMA
    remaining, update = pl.pallas_call(
        kernel,
        name="gather_product_low",
        out_shape=tuple(pltpu.VMEM(shape, BF16) for shape in shapes),
        in_specs=[any_space] * 10,
        out_specs=(pl.BlockSpec(memory_space=pltpu.VMEM),) * 2,
        scratch_shapes=[
            pltpu.VMEM((2, 8, 1024, 256), BF16),
            pltpu.VMEM((2, 8, 256, 256), F32),
            pltpu.VMEM((2, 8, 32, 256), F32),
            pltpu.VMEM((1024, 256), BF16),
            pltpu.VMEM((8, 352, 128), BF16),
            pltpu.VMEM((4096, 256), BF16),
            pltpu.VMEM((2, 8, 8, 128), F32),
            pltpu.VMEM((2, 8, 8, 128), F32),
            *[pltpu.VMEM(c.shape, c.dtype) for c in consts],
            dma((2, 4, 8)),
            dma((4, 16)),
            dma((4, 16)),
            dma((2, 8)),
            dma((2, 4)),
            dma((4,)),
            dma((4,)),
            dma((2,)),
            dma((10,)),
        ],
        compiler_params=pltpu.CompilerParams(
            collective_id=0, has_side_effects=True, vmem_limit_bytes=44 * 1024 * 1024
        ),
        cost_estimate=pl.CostEstimate(flops=2 * 1024 * 4096 * 352, bytes_accessed=5 << 20, transcendentals=512 * 256),
    )(*[pltpu.with_memory_space_constraint(x, pltpu.HBM) for x in (activations, out_grads, momentum[0], *consts)])
    remaining, update = pl.pallas_call(
        store_kernel,
        name="store",
        out_shape=tuple(pltpu.HBM(shape, BF16) for shape in shapes),
        in_specs=[any_space] * 2,
        out_specs=(any_space, any_space),
        scratch_shapes=[dma((5,))],
    )(*[pltpu.with_memory_space_constraint(x, pltpu.VMEM) for x in (remaining, update)])
    return remaining[None], update


def solution(mesh):
    return jax.shard_map(
        body,
        mesh=mesh,
        in_specs=(P(("dp", "mp"), None), P("dp", "mp"), P("dp", None, "mp")),
        out_specs=(P("dp", None, "mp"), P("dp", "mp")),
        check_vma=False,
    )
```

```python
import functools

import jax
import jax.numpy as jnp
import ml_dtypes
import numpy as np
from jax import lax
from jax.experimental import pallas as pl
from jax.experimental.pallas import tpu as pltpu
from jax.sharding import PartitionSpec as P

BETA = 0.9
EPSILON = 1e-06
MESH = pl.DeviceIdType.MESH
NZ = 16
NB = 5
UP, DOWN = 0, 1
F32, BF16 = jnp.float32, jnp.bfloat16


def low_basis():
    order = np.arange(8)[:, None]
    position = np.arange(64)[None, :]
    factor = np.where(order == 0, 0.125, np.sqrt(2.0 / 64.0))
    return (factor * np.cos(np.pi * (2 * position + 1) * order / 128.0)).astype(np.float32)


def pieces_np(x):
    one = x.astype(ml_dtypes.bfloat16)
    rest = x - one.astype(np.float32)
    two = rest.astype(ml_dtypes.bfloat16)
    three = (rest - two.astype(np.float32)).astype(ml_dtypes.bfloat16)
    return one, two, three


def constants():
    b = low_basis()
    kb = np.kron(np.eye(4, dtype=np.float32), b)
    k1, k2, k3 = pieces_np(kb)
    zero = np.zeros_like(k1)
    first = np.concatenate([k1, k2, k3], 0)
    wide = [np.tile(k.T, (1, 4)) for k in (k1, k1, k1, k2, k2, k3)]
    to_low = np.concatenate(wide, 0)
    from_low = np.concatenate([k1, k1, k1, k2, k2, k3, zero, zero], 0)
    columns = np.concatenate([k.T for k in (k1, k1, k1, k2, k2, k3)], 1)
    tall = np.concatenate([np.tile(k, (4, 1)) for k in (k1, k1, k1, k2, k2, k3)], 0)
    eight = np.tile(b.T, (4, 1))
    ones = np.kron(np.eye(16, dtype=np.float32), np.ones((8, 8), np.float32)).astype(ml_dtypes.bfloat16)
    return first, to_low, from_low, columns, tall, eight, ones


def pieces(x):
    one = x.astype(BF16)
    rest = x - one.astype(F32)
    two = rest.astype(BF16)
    three = (rest - two.astype(F32)).astype(BF16)
    return one, two, three


def dot(a, b):
    return lax.dot_general(a, b, (((1,), (0,)), ((), ())), preferred_element_type=F32)


def update_rows(average, eight, ones, tall):
    square = jnp.sum(average * average, axis=0, keepdims=True)
    s1, s2, s3 = pieces(jnp.broadcast_to(square, (8, 128)))
    power = (dot(s1, ones[...]) + dot(s2, ones[...]) + dot(s3, ones[...])) * (1.0 / 4096.0)
    scaled = average / jnp.sqrt(power + EPSILON)
    spread = jnp.dot(eight[...], scaled, precision=lax.Precision.HIGHEST, preferred_element_type=F32)
    row_group = lax.broadcasted_iota(jnp.int32, (256, 128), 0) // 64
    lanes = lax.broadcasted_iota(jnp.int32, (256, 128), 1) // 32
    spread = jnp.where(row_group == lanes, spread, 0.0)
    s1, s2, s3 = pieces(spread)
    shared = dot(jnp.concatenate([s1, s2, s3, s1, s2, s1], 1), tall[...])
    return jnp.tanh(shared).T.astype(BF16)


def kernel(
    act, grads, mom, c_first, c_to_low, c_from_low, c_columns, c_tall, c_eight, c_ones,
    rem, upd, average, tall, eight, ones,
    buf, acc, acc_low, g_in, g_t, m_in, low_out, low_in,
    first, to_low, from_low, columns,
    zr, yr, cr, lr, zs, ys, cs, ls, local,
):
    group, lane_id = lax.axis_index("dp"), lax.axis_index("mp")
    z, y, core = lane_id // 4, (lane_id // 2) % 2, lane_id % 2

    def at(zz, yy, cc):
        return {"mp": (zz * 2 + yy) * 2 + cc}

    hop = (at((z + 1) % NZ, y, core), at((z + NZ - 1) % NZ, y, core))
    pair, twin = at(z, 1 - y, core), at(z, y, 1 - core)

    tiles = {"B": (0, NB), "A": (NB, 8 - NB)}
    last = {("B", UP): 8, ("B", DOWN): 7, ("A", UP): 7, ("A", DOWN): 8}
    tall_rows = {"B": 16, "A": 32}
    OWN = 960

    def number(h, kind):
        return h * 2 + (0 if kind == "B" else 1)

    def level(direction, s):
        if isinstance(s, int) and s == 8:
            return 896, 14
        row = (s - 1) * 128 + (64 if direction == DOWN else 0)
        return (row if isinstance(row, int) else pl.multiple_of(row, 64)), (s - 1) * 2 + direction

    def part(h, kind, row, rows):
        begin, count = tiles[kind]
        return buf.at[h, pl.ds(begin, count), pl.ds(row, rows)]

    def remote(src, dst, send, recv, device):
        return pltpu.make_async_remote_copy(
            src_ref=src, dst_ref=dst, send_sem=send, recv_sem=recv, device_id=device, device_id_type=MESH
        )

    def z_copy(h, kind, direction, s):
        n, rows = number(h, kind), tall_rows[kind]
        src = OWN if isinstance(s, int) and s == 1 else level(direction, s - 1)[0]
        dst, _ = level(direction, s)
        return remote(
            part(h, kind, src, rows), part(h, kind, dst, rows),
            zs.at[direction, n], zr.at[direction, n, s - 1], hop[direction],
        )

    def y_copy(h, kind, row, index):
        n = number(h, kind)
        return remote(
            part(h, kind, row, 16), part(h, kind, row + 16, 16), ys.at[n], yr.at[n, index], pair
        )

    def c_copy(h, kind, row, index):
        n = number(h, kind)
        return remote(
            part(h, kind, row, 32), part(h, kind, row + 32, 32), cs.at[n], cr.at[n, index], twin
        )

    def directions(kind, s):
        if not isinstance(s, int):
            return (UP, DOWN)
        return tuple(d for d in (UP, DOWN) if 1 <= s <= last[kind, d])

    def on_z(h, kind, s):
        for direction in directions(kind, s):
            z_copy(h, kind, direction, s).wait_recv()
            if not isinstance(s, int) or s < last[kind, direction]:
                z_copy(h, kind, direction, s + 1).start()
            row, index = level(direction, s)
            (y_copy if kind == "B" else c_copy)(h, kind, row, index).start()

    def on_y(h, kind, s):
        for direction in directions(kind, s):
            row, index = level(direction, s)
            y_copy(h, kind, row, index).wait_recv()
            c_copy(h, kind, row, index).start()

    def add_product(h, kind, s):
        for direction in directions(kind, s):
            row, index = level(direction, s)
            c_copy(h, kind, row, index).wait_recv()
        if isinstance(s, int) and s == 8:
            c_copy(h, kind, OWN, 15).wait_recv()
        begin, count = tiles[kind]
        rows = (s - 1) * 128
        rows = rows if isinstance(rows, int) else pl.multiple_of(rows, 128)
        left = g_t[s - 1]

        for d in range(begin, begin + count):
            product = dot(left, buf[h, d, pl.ds(rows, 128), :])
            acc[h, d] += product[:256]
            acc_low[h, d] += product[256:288] + product[288:320] + product[320:352]

    def start_sum(h, kind):
        begin, count = tiles[kind]

        for d in range(begin, begin + count):
            row = d * 512 + h * 256
            turned = m_in[row : row + 256, :].T
            acc[h, d] = BETA * turned.astype(F32)
            product = dot(first[...], turned)
            acc_low[h, d] = BETA * (product[:32] + product[32:64] + product[64:])

    def by_lanes(a, b, c, d):
        g = lax.broadcasted_iota(jnp.int32, a.shape, 1) // 32
        return jnp.where(g == 0, a, jnp.where(g == 1, b, jnp.where(g == 2, c, d)))

    low_keep = {}

    def low_of(h, kind):
        begin, count = tiles[kind]
        x = acc_low[h, begin : begin + count].reshape(count * 32, 256)
        x1, x2, x3 = pieces(x)
        low = dot(jnp.concatenate([x1, x2, x3, x1, x2, x1], 1), to_low[...])
        low_keep[h, kind] = low
        for i in range(count):
            d = begin + i
            block = [low[i * 32 + 8 * k : i * 32 + 8 * k + 8] for k in range(4)]
            low_out[h, d] = by_lanes(*block)
        for i in range(count):
            d = begin + i
            slot = (group - d + 8) % 8

            @pl.when(d != group)
            def _(d=d, slot=slot):
                remote(low_out.at[h, d], low_in.at[h, slot], ls.at[h], lr.at[h, slot], {"dp": d}).start()

    def remaining_of(h, kind):
        begin, count = tiles[kind]
        l1, l2, l3 = pieces(low_keep[h, kind])
        zero = jnp.zeros_like(l1)
        left = jnp.concatenate([by_lanes(l1, l2, l3, l1), by_lanes(l2, l1, zero, zero)], 1)
        w = dot(left, from_low[...])
        for i in range(count):
            d = begin + i
            w1, w2, w3 = pieces(w[i * 32 : i * 32 + 32])
            expanded = dot(columns[...], jnp.concatenate([w1, w2, w3, w1, w2, w1], 0))
            rest = (acc[h, d] - expanded).T.astype(BF16)
            row = d * 512 + h * 256
            rem[row : row + 256, :] = rest

    def average_of(h):
        for k in range(1, 8):
            remote(low_out.at[h, 0], low_in.at[h, k], ls.at[h], lr.at[h, k], {"dp": group}).wait_recv()
        total = low_out[h, group]
        for k in range(1, 8):
            total = total + low_in[h, k]
        return total * 0.125

    barrier = pltpu.get_barrier_semaphore()
    for device in (*hop, pair, twin):
        pl.semaphore_signal(barrier, inc=1, device_id=device, device_id_type=MESH)
    for k in range(1, 8):
        pl.semaphore_signal(barrier, inc=1, device_id={"dp": (group + k) % 8}, device_id_type=MESH)

    for h in range(2):
        for d in range(8):
            pltpu.make_async_copy(
                act.at[:, pl.ds(d * 512 + h * 256, 256)], buf.at[h, d, pl.ds(OWN, 16)], local.at[0]
            ).start()

    pl.semaphore_wait(barrier, 11)

    own_all = buf.at[:, :, pl.ds(OWN, 16)]
    pltpu.make_async_copy(own_all, own_all, local.at[0]).wait()

    y_copy(0, "A", OWN, 15).start()
    y_copy(1, "A", OWN, 15).start()
    for h in range(2):
        for direction in (UP, DOWN):
            z_copy(h, "B", direction, 1).start()
    y_copy(0, "B", OWN, 15).start()
    y_copy(1, "B", OWN, 15).start()

    def own_rows(zz, yo, co):
        m = (zz * 2 + (y + yo) % 2) * 2 + (core + co) % 2
        return pl.multiple_of(m * 16, 16)

    for co in range(2):
        for yo in range(2):
            pltpu.make_async_copy(
                grads.at[pl.ds(own_rows(z, yo, co), 16)], g_in.at[pl.ds(OWN + co * 32 + yo * 16, 16)], local.at[1]
            ).start()

            @pl.loop(0, 15)
            def _(k, co=co, yo=yo):
                s = k // 2 + 1
                zz = (z + NZ - s + (k % 2) * 2 * s) % NZ
                row = pl.multiple_of(k * 64 + co * 32 + yo * 16, 16)
                pltpu.make_async_copy(
                    grads.at[pl.ds(own_rows(zz, yo, co), 16)], g_in.at[pl.ds(row, 16)], local.at[1]
                ).start()

    constant = (
        (c_first, first), (c_to_low, to_low), (c_from_low, from_low), (c_columns, columns),
        (c_tall, tall), (c_eight, eight), (c_ones, ones),
    )
    const_copies = [
        pltpu.make_async_copy(src, dst, local.at[3 + i]) for i, (src, dst) in enumerate(constant)
    ]
    for copy in const_copies:
        copy.start()
    pltpu.make_async_copy(mom, m_in, local.at[2]).start()

    def both_columns(h):
        y_copy(h, "A", OWN, 15).wait_recv()
        for direction in (UP, DOWN):
            z_copy(h, "A", direction, 1).start()
        c_copy(h, "A", OWN, 15).start()

    def own_column(h):
        y_copy(h, "B", OWN, 15).wait_recv()
        c_copy(h, "B", OWN, 15).start()

    slot = (
        (on_z, 1, "A", 2), (add_product, 1, "A", 3), (on_z, 0, "B", 0), (on_y, 0, "B", 1), (add_product, 1, "B", 2),
        (add_product, 0, "A", 1), (on_z, 1, "B", 0), (on_z, 0, "A", 0), (on_y, 1, "B", 1), (add_product, 0, "B", 1),
    )

    def run_slot(t):
        for task, h, kind, lag in slot:
            if not isinstance(t, int) or 1 <= t - lag <= 8:
                task(h, kind, t - lag)
                if task is add_product and isinstance(t, int) and t - lag == 8:
                    low_of(h, kind)

    both_columns(0)
    run_slot(1)
    both_columns(1)

    const_copies[0].wait()
    pltpu.make_async_copy(g_in, g_in, local.at[1]).wait()

    for s in range(8):
        turned = g_in[s * 128 : s * 128 + 128, :].T
        g_t[s, :256] = turned
        product = dot(first[...], turned)
        for i, piece in enumerate(pieces(product[:32] + product[32:64] + product[64:])):
            g_t[s, 256 + 32 * i : 288 + 32 * i] = piece

    pltpu.make_async_copy(m_in, m_in, local.at[2]).wait()
    start_sum(0, "A")
    start_sum(0, "B")
    run_slot(2)
    own_column(0)
    own_column(1)
    start_sum(1, "B")
    start_sum(1, "A")
    run_slot(3)

    @pl.loop(4, 7)
    def _(t):
        run_slot(t)

    run_slot(7)
    run_slot(8)
    for copy in const_copies[1:]:
        copy.wait()
    run_slot(9)
    run_slot(10)
    run_slot(11)
    remaining_of(0, "A")
    remaining_of(0, "B")
    upd[...] = update_rows(average_of(0), eight, ones, tall)
    remaining_of(1, "B")
    remaining_of(1, "A")
    average[...] = average_of(1)

    for h in range(2):
        for kind in ("B", "A"):
            n, rows = number(h, kind), tall_rows[kind]
            for direction in (UP, DOWN):
                sent = part(h, kind, 0, rows * last[kind, direction])
                remote(sent, sent, zs.at[direction, n], zr.at[direction, n, 0], hop[direction]).wait_send()
            sent = part(h, kind, 0, 256 if kind == "B" else 16)
            remote(sent, sent, ys.at[n], yr.at[n, 0], pair).wait_send()
            sent = part(h, kind, 0, 512)
            remote(sent, sent, cs.at[n], cr.at[n, 0], twin).wait_send()
        sent = low_out.at[h, pl.ds(0, 7)]
        remote(sent, sent, ls.at[h], lr.at[h, 0], {"dp": group}).wait_send()


def store_kernel(rem, upd, average, tall, eight, ones, rem_out, upd_out, later, sem):
    copies = [pltpu.make_async_copy(upd, upd_out.at[pl.ds(0, 256)], sem.at[0])]
    for i in range(4):
        rows = pl.ds(i * 1024, 1024)
        copies.append(pltpu.make_async_copy(rem.at[rows], rem_out.at[rows], sem.at[2 + i]))
    for copy in copies:
        copy.start()
    later[...] = update_rows(average[...], eight, ones, tall)
    copies.append(pltpu.make_async_copy(later, upd_out.at[pl.ds(256, 256)], sem.at[1]))
    copies[-1].start()
    for copy in copies:
        copy.wait()


def body(activations, out_grads, momentum):
    consts = [jnp.asarray(c) for c in constants()]
    kept = (((4096, 256), BF16), ((256, 256), BF16), ((8, 128), F32)) + tuple((c.shape, c.dtype) for c in consts[4:])
    any_space = pl.BlockSpec(memory_space=pl.ANY)
    vmem_space = pl.BlockSpec(memory_space=pltpu.VMEM)
    dma = pltpu.SemaphoreType.DMA
    results = pl.pallas_call(
        kernel,
        name="gather_product_low",
        out_shape=tuple(pltpu.VMEM(shape, dtype) for shape, dtype in kept),
        in_specs=[any_space] * 10,
        out_specs=(vmem_space,) * 6,
        scratch_shapes=[
            pltpu.VMEM((2, 8, 1024, 256), BF16),
            pltpu.VMEM((2, 8, 256, 256), F32),
            pltpu.VMEM((2, 8, 32, 256), F32),
            pltpu.VMEM((1024, 256), BF16),
            pltpu.VMEM((8, 352, 128), BF16),
            pltpu.VMEM((4096, 256), BF16),
            pltpu.VMEM((2, 8, 8, 128), F32),
            pltpu.VMEM((2, 8, 8, 128), F32),
            *[pltpu.VMEM(c.shape, c.dtype) for c in consts[:4]],
            dma((2, 4, 8)),
            dma((4, 16)),
            dma((4, 16)),
            dma((2, 8)),
            dma((2, 4)),
            dma((4,)),
            dma((4,)),
            dma((2,)),
            dma((10,)),
        ],
        compiler_params=pltpu.CompilerParams(
            collective_id=0, has_side_effects=True, vmem_limit_bytes=44 * 1024 * 1024
        ),
        cost_estimate=pl.CostEstimate(flops=2 * 1024 * 4096 * 352, bytes_accessed=5 << 20, transcendentals=512 * 256),
    )(*[pltpu.with_memory_space_constraint(x, pltpu.HBM) for x in (activations, out_grads, momentum[0], *consts)])
    remaining, update = pl.pallas_call(
        store_kernel,
        name="store",
        out_shape=(pltpu.HBM((4096, 256), BF16), pltpu.HBM((512, 256), BF16)),
        in_specs=[vmem_space] * 6,
        out_specs=(any_space, any_space),
        scratch_shapes=[pltpu.VMEM((256, 256), BF16), dma((6,))],
    )(*[pltpu.with_memory_space_constraint(x, pltpu.VMEM) for x in results])
    return remaining[None], update


def solution(mesh):
    return jax.shard_map(
        body,
        mesh=mesh,
        in_specs=(P(("dp", "mp"), None), P("dp", "mp"), P("dp", None, "mp")),
        out_specs=(P("dp", None, "mp"), P("dp", "mp")),
        check_vma=False,
    )
```

```python
import functools

import jax
import jax.numpy as jnp
import ml_dtypes
import numpy as np
from jax import lax
from jax.experimental import pallas as pl
from jax.experimental.pallas import tpu as pltpu
from jax.sharding import PartitionSpec as P

BETA = 0.9
EPSILON = 1e-06
MESH = pl.DeviceIdType.MESH
NZ = 16
NB = 5
UP, DOWN = 0, 1
F32, BF16 = jnp.float32, jnp.bfloat16


def low_basis():
    order = np.arange(8)[:, None]
    position = np.arange(64)[None, :]
    factor = np.where(order == 0, 0.125, np.sqrt(2.0 / 64.0))
    return (factor * np.cos(np.pi * (2 * position + 1) * order / 128.0)).astype(np.float32)


def pieces_np(x):
    one = x.astype(ml_dtypes.bfloat16)
    rest = x - one.astype(np.float32)
    two = rest.astype(ml_dtypes.bfloat16)
    three = (rest - two.astype(np.float32)).astype(ml_dtypes.bfloat16)
    return one, two, three


def constants():
    b = low_basis()
    kb = np.kron(np.eye(4, dtype=np.float32), b)
    k1, k2, k3 = pieces_np(kb)
    zero = np.zeros_like(k1)
    first = np.concatenate([k1, k2, k3], 0)
    wide = [np.tile(k.T, (1, 4)) for k in (k1, k1, k1, k2, k2, k3)]
    to_low = np.concatenate(wide, 0)
    from_low = np.concatenate([k1, k1, k1, k2, k2, k3, zero, zero], 0)
    columns = np.concatenate([k.T for k in (k1, k1, k1, k2, k2, k3)], 1)
    tall = np.concatenate([np.tile(k, (4, 1)) for k in (k1, k1, k1, k2, k2, k3)], 0)
    eight = np.tile(b.T, (4, 1))
    ones = np.kron(np.eye(16, dtype=np.float32), np.ones((8, 8), np.float32)).astype(ml_dtypes.bfloat16)
    return first, to_low, from_low, columns, tall, eight, ones


def pieces(x):
    one = x.astype(BF16)
    rest = x - one.astype(F32)
    two = rest.astype(BF16)
    three = (rest - two.astype(F32)).astype(BF16)
    return one, two, three


def dot(a, b):
    return lax.dot_general(a, b, (((1,), (0,)), ((), ())), preferred_element_type=F32)


def update_rows(average, eight, ones, tall):
    square = jnp.sum(average * average, axis=0, keepdims=True)
    s1, s2, s3 = pieces(jnp.broadcast_to(square, (8, 128)))
    power = (dot(s1, ones[...]) + dot(s2, ones[...]) + dot(s3, ones[...])) * (1.0 / 4096.0)
    scaled = average / jnp.sqrt(power + EPSILON)
    spread = jnp.dot(eight[...], scaled, precision=lax.Precision.HIGHEST, preferred_element_type=F32)
    row_group = lax.broadcasted_iota(jnp.int32, (256, 128), 0) // 64
    lanes = lax.broadcasted_iota(jnp.int32, (256, 128), 1) // 32
    spread = jnp.where(row_group == lanes, spread, 0.0)
    s1, s2, s3 = pieces(spread)
    shared = dot(jnp.concatenate([s1, s2, s3, s1, s2, s1], 1), tall[...])
    return jnp.tanh(shared).T.astype(BF16)


def kernel(
    act, grads, mom, c_first, c_to_low, c_from_low, c_columns, c_tall, c_eight, c_ones,
    rem, upd, average, tall, eight, ones,
    buf, acc, acc_low, g_in, g_t, m_in, low_out, low_in,
    first, to_low, from_low, columns,
    zr, yr, cr, lr, zs, ys, cs, ls, local, met, met_all,
):
    group, lane_id = lax.axis_index("dp"), lax.axis_index("mp")
    z, y, core = lane_id // 4, (lane_id // 2) % 2, lane_id % 2

    def at(zz, yy, cc):
        return {"mp": (zz * 2 + yy) * 2 + cc}

    hop = (at((z + 1) % NZ, y, core), at((z + NZ - 1) % NZ, y, core))
    pair, twin = at(z, 1 - y, core), at(z, y, 1 - core)

    tiles = {"B": (0, NB), "A": (NB, 8 - NB)}
    last = {("B", UP): 8, ("B", DOWN): 7, ("A", UP): 7, ("A", DOWN): 8}
    tall_rows = {"B": 16, "A": 32}
    OWN = 960

    def number(h, kind):
        return h * 2 + (0 if kind == "B" else 1)

    def level(direction, s):
        if isinstance(s, int) and s == 8:
            return 896, 14
        row = (s - 1) * 128 + (64 if direction == DOWN else 0)
        return (row if isinstance(row, int) else pl.multiple_of(row, 64)), (s - 1) * 2 + direction

    def part(h, kind, row, rows):
        begin, count = tiles[kind]
        return buf.at[h, pl.ds(begin, count), pl.ds(row, rows)]

    def remote(src, dst, send, recv, device):
        return pltpu.make_async_remote_copy(
            src_ref=src, dst_ref=dst, send_sem=send, recv_sem=recv, device_id=device, device_id_type=MESH
        )

    def z_copy(h, kind, direction, s):
        n, rows = number(h, kind), tall_rows[kind]
        src = OWN if isinstance(s, int) and s == 1 else level(direction, s - 1)[0]
        dst, _ = level(direction, s)
        return remote(
            part(h, kind, src, rows), part(h, kind, dst, rows),
            zs.at[direction, n], zr.at[direction, n, s - 1], hop[direction],
        )

    def y_copy(h, kind, row, index):
        n = number(h, kind)
        return remote(
            part(h, kind, row, 16), part(h, kind, row + 16, 16), ys.at[n], yr.at[n, index], pair
        )

    def c_copy(h, kind, row, index):
        n = number(h, kind)
        return remote(
            part(h, kind, row, 32), part(h, kind, row + 32, 32), cs.at[n], cr.at[n, index], twin
        )

    def directions(kind, s):
        if not isinstance(s, int):
            return (UP, DOWN)
        return tuple(d for d in (UP, DOWN) if 1 <= s <= last[kind, d])

    def on_z(h, kind, s):
        for direction in directions(kind, s):
            z_copy(h, kind, direction, s).wait_recv()
            if not isinstance(s, int) or s < last[kind, direction]:
                z_copy(h, kind, direction, s + 1).start()
            row, index = level(direction, s)
            (y_copy if kind == "B" else c_copy)(h, kind, row, index).start()

    def on_y(h, kind, s):
        for direction in directions(kind, s):
            row, index = level(direction, s)
            y_copy(h, kind, row, index).wait_recv()
            c_copy(h, kind, row, index).start()

    def add_product(h, kind, s):
        for direction in directions(kind, s):
            row, index = level(direction, s)
            c_copy(h, kind, row, index).wait_recv()
        if isinstance(s, int) and s == 8:
            c_copy(h, kind, OWN, 15).wait_recv()
        begin, count = tiles[kind]
        rows = (s - 1) * 128
        rows = rows if isinstance(rows, int) else pl.multiple_of(rows, 128)
        left = g_t[s - 1]

        for d in range(begin, begin + count):
            product = dot(left, buf[h, d, pl.ds(rows, 128), :])
            acc[h, d] += product[:256]
            acc_low[h, d] += product[256:288] + product[288:320] + product[320:352]

    def start_sum(h, kind):
        begin, count = tiles[kind]

        for d in range(begin, begin + count):
            row = d * 512 + h * 256
            turned = m_in[row : row + 256, :].T
            acc[h, d] = BETA * turned.astype(F32)
            product = dot(first[...], turned)
            acc_low[h, d] = BETA * (product[:32] + product[32:64] + product[64:])

    def by_lanes(a, b, c, d):
        g = lax.broadcasted_iota(jnp.int32, a.shape, 1) // 32
        return jnp.where(g == 0, a, jnp.where(g == 1, b, jnp.where(g == 2, c, d)))

    low_keep = {}

    def low_of(h, kind):
        begin, count = tiles[kind]
        x = acc_low[h, begin : begin + count].reshape(count * 32, 256)
        x1, x2, x3 = pieces(x)
        low = dot(jnp.concatenate([x1, x2, x3, x1, x2, x1], 1), to_low[...])
        low_keep[h, kind] = low
        for i in range(count):
            d = begin + i
            block = [low[i * 32 + 8 * k : i * 32 + 8 * k + 8] for k in range(4)]
            low_out[h, d] = by_lanes(*block)
        for i in range(count):
            d = begin + i
            slot = (group - d + 8) % 8

            @pl.when(d != group)
            def _(d=d, slot=slot):
                remote(low_out.at[h, d], low_in.at[h, slot], ls.at[h], lr.at[h, slot], {"dp": d}).start()

    def remaining_of(h, kind):
        begin, count = tiles[kind]
        l1, l2, l3 = pieces(low_keep[h, kind])
        zero = jnp.zeros_like(l1)
        left = jnp.concatenate([by_lanes(l1, l2, l3, l1), by_lanes(l2, l1, zero, zero)], 1)
        w = dot(left, from_low[...])
        for i in range(count):
            d = begin + i
            w1, w2, w3 = pieces(w[i * 32 : i * 32 + 32])
            expanded = dot(columns[...], jnp.concatenate([w1, w2, w3, w1, w2, w1], 0))
            rest = (acc[h, d] - expanded).T.astype(BF16)
            row = d * 512 + h * 256
            rem[row : row + 256, :] = rest

    def average_of(h):
        for k in range(1, 8):
            remote(low_out.at[h, 0], low_in.at[h, k], ls.at[h], lr.at[h, k], {"dp": group}).wait_recv()
        total = low_out[h, group]
        for k in range(1, 8):
            total = total + low_in[h, k]
        return total * 0.125

    barrier = pltpu.get_barrier_semaphore()
    for device in (*hop, pair, twin):
        pl.semaphore_signal(barrier, inc=1, device_id=device, device_id_type=MESH)
    row_start = (group // 4) * 4
    near = ({"dp": row_start + (group + 1) % 4}, {"dp": row_start + (group + 3) % 4}, {"dp": (group + 4) % 8})
    for device in near:
        pl.semaphore_signal(barrier, inc=1, device_id=device, device_id_type=MESH)

    for h in range(2):
        for d in range(8):
            pltpu.make_async_copy(
                act.at[:, pl.ds(d * 512 + h * 256, 256)], buf.at[h, d, pl.ds(OWN, 16)], local.at[0]
            ).start()

    pl.semaphore_wait(barrier, 7)

    own_all = buf.at[:, :, pl.ds(OWN, 16)]
    pltpu.make_async_copy(own_all, own_all, local.at[0]).wait()

    y_copy(0, "A", OWN, 15).start()
    y_copy(1, "A", OWN, 15).start()
    for h in range(2):
        for direction in (UP, DOWN):
            z_copy(h, "B", direction, 1).start()
    y_copy(0, "B", OWN, 15).start()
    y_copy(1, "B", OWN, 15).start()

    def own_rows(zz, yo, co):
        m = (zz * 2 + (y + yo) % 2) * 2 + (core + co) % 2
        return pl.multiple_of(m * 16, 16)

    for co in range(2):
        for yo in range(2):
            pltpu.make_async_copy(
                grads.at[pl.ds(own_rows(z, yo, co), 16)], g_in.at[pl.ds(OWN + co * 32 + yo * 16, 16)], local.at[1]
            ).start()

            @pl.loop(0, 15)
            def _(k, co=co, yo=yo):
                s = k // 2 + 1
                zz = (z + NZ - s + (k % 2) * 2 * s) % NZ
                row = pl.multiple_of(k * 64 + co * 32 + yo * 16, 16)
                pltpu.make_async_copy(
                    grads.at[pl.ds(own_rows(zz, yo, co), 16)], g_in.at[pl.ds(row, 16)], local.at[1]
                ).start()

    constant = (
        (c_first, first), (c_to_low, to_low), (c_from_low, from_low), (c_columns, columns),
        (c_tall, tall), (c_eight, eight), (c_ones, ones),
    )
    const_copies = [
        pltpu.make_async_copy(src, dst, local.at[3 + i]) for i, (src, dst) in enumerate(constant)
    ]
    for copy in const_copies:
        copy.start()
    pltpu.make_async_copy(mom, m_in, local.at[2]).start()

    def both_columns(h):
        y_copy(h, "A", OWN, 15).wait_recv()
        for direction in (UP, DOWN):
            z_copy(h, "A", direction, 1).start()
        c_copy(h, "A", OWN, 15).start()

    def own_column(h):
        y_copy(h, "B", OWN, 15).wait_recv()
        c_copy(h, "B", OWN, 15).start()

    slot = (
        (on_z, 1, "A", 2), (add_product, 1, "A", 3), (on_z, 0, "B", 0), (on_y, 0, "B", 1), (add_product, 1, "B", 2),
        (add_product, 0, "A", 1), (on_z, 1, "B", 0), (on_z, 0, "A", 0), (on_y, 1, "B", 1), (add_product, 0, "B", 1),
    )

    def run_slot(t):
        for task, h, kind, lag in slot:
            if not isinstance(t, int) or 1 <= t - lag <= 8:
                task(h, kind, t - lag)
                if task is add_product and isinstance(t, int) and t - lag == 8:
                    low_of(h, kind)

    both_columns(0)
    run_slot(1)
    both_columns(1)

    const_copies[0].wait()
    pltpu.make_async_copy(g_in, g_in, local.at[1]).wait()

    for s in range(8):
        turned = g_in[s * 128 : s * 128 + 128, :].T
        g_t[s, :256] = turned
        product = dot(first[...], turned)
        for i, piece in enumerate(pieces(product[:32] + product[32:64] + product[64:])):
            g_t[s, 256 + 32 * i : 288 + 32 * i] = piece

    pltpu.make_async_copy(m_in, m_in, local.at[2]).wait()
    start_sum(0, "A")
    start_sum(0, "B")
    for device in near:
        pl.semaphore_signal(met, inc=1, device_id=device, device_id_type=MESH)
    run_slot(2)
    own_column(0)
    own_column(1)
    start_sum(1, "B")
    start_sum(1, "A")
    run_slot(3)

    @pl.loop(4, 7)
    def _(t):
        run_slot(t)

    pl.semaphore_wait(met, 3)
    pl.semaphore_signal(met_all, inc=1, device_id=near[2], device_id_type=MESH)
    run_slot(7)
    run_slot(8)
    pl.semaphore_wait(met_all, 1)
    for copy in const_copies[1:]:
        copy.wait()
    run_slot(9)
    run_slot(10)
    run_slot(11)
    remaining_of(0, "A")
    remaining_of(0, "B")
    upd[...] = update_rows(average_of(0), eight, ones, tall)
    remaining_of(1, "B")
    remaining_of(1, "A")
    average[...] = average_of(1)

    for h in range(2):
        for kind in ("B", "A"):
            n, rows = number(h, kind), tall_rows[kind]
            for direction in (UP, DOWN):
                sent = part(h, kind, 0, rows * last[kind, direction])
                remote(sent, sent, zs.at[direction, n], zr.at[direction, n, 0], hop[direction]).wait_send()
            sent = part(h, kind, 0, 256 if kind == "B" else 16)
            remote(sent, sent, ys.at[n], yr.at[n, 0], pair).wait_send()
            sent = part(h, kind, 0, 512)
            remote(sent, sent, cs.at[n], cr.at[n, 0], twin).wait_send()
        sent = low_out.at[h, pl.ds(0, 7)]
        remote(sent, sent, ls.at[h], lr.at[h, 0], {"dp": group}).wait_send()


def store_kernel(rem, upd, average, tall, eight, ones, rem_out, upd_out, later, sem):
    copies = [pltpu.make_async_copy(upd, upd_out.at[pl.ds(0, 256)], sem.at[0])]
    for i in range(4):
        rows = pl.ds(i * 1024, 1024)
        copies.append(pltpu.make_async_copy(rem.at[rows], rem_out.at[rows], sem.at[2 + i]))
    for copy in copies:
        copy.start()
    later[...] = update_rows(average[...], eight, ones, tall)
    copies.append(pltpu.make_async_copy(later, upd_out.at[pl.ds(256, 256)], sem.at[1]))
    copies[-1].start()
    for copy in copies:
        copy.wait()


def body(activations, out_grads, momentum):
    consts = [jnp.asarray(c) for c in constants()]
    kept = (((4096, 256), BF16), ((256, 256), BF16), ((8, 128), F32)) + tuple((c.shape, c.dtype) for c in consts[4:])
    any_space = pl.BlockSpec(memory_space=pl.ANY)
    vmem_space = pl.BlockSpec(memory_space=pltpu.VMEM)
    dma = pltpu.SemaphoreType.DMA
    results = pl.pallas_call(
        kernel,
        name="gather_product_low",
        out_shape=tuple(pltpu.VMEM(shape, dtype) for shape, dtype in kept),
        in_specs=[any_space] * 10,
        out_specs=(vmem_space,) * 6,
        scratch_shapes=[
            pltpu.VMEM((2, 8, 1024, 256), BF16),
            pltpu.VMEM((2, 8, 256, 256), F32),
            pltpu.VMEM((2, 8, 32, 256), F32),
            pltpu.VMEM((1024, 256), BF16),
            pltpu.VMEM((8, 352, 128), BF16),
            pltpu.VMEM((4096, 256), BF16),
            pltpu.VMEM((2, 8, 8, 128), F32),
            pltpu.VMEM((2, 8, 8, 128), F32),
            *[pltpu.VMEM(c.shape, c.dtype) for c in consts[:4]],
            dma((2, 4, 8)),
            dma((4, 16)),
            dma((4, 16)),
            dma((2, 8)),
            dma((2, 4)),
            dma((4,)),
            dma((4,)),
            dma((2,)),
            dma((10,)),
            pltpu.SemaphoreType.REGULAR,
            pltpu.SemaphoreType.REGULAR,
        ],
        compiler_params=pltpu.CompilerParams(
            collective_id=0, has_side_effects=True, vmem_limit_bytes=44 * 1024 * 1024
        ),
        cost_estimate=pl.CostEstimate(flops=2 * 1024 * 4096 * 352, bytes_accessed=5 << 20, transcendentals=512 * 256),
    )(*[pltpu.with_memory_space_constraint(x, pltpu.HBM) for x in (activations, out_grads, momentum[0], *consts)])
    remaining, update = pl.pallas_call(
        store_kernel,
        name="store",
        out_shape=(pltpu.HBM((4096, 256), BF16), pltpu.HBM((512, 256), BF16)),
        in_specs=[vmem_space] * 6,
        out_specs=(any_space, any_space),
        scratch_shapes=[pltpu.VMEM((256, 256), BF16), dma((6,))],
    )(*[pltpu.with_memory_space_constraint(x, pltpu.VMEM) for x in results])
    return remaining[None], update


def solution(mesh):
    return jax.shard_map(
        body,
        mesh=mesh,
        in_specs=(P(("dp", "mp"), None), P("dp", "mp"), P("dp", None, "mp")),
        out_specs=(P("dp", None, "mp"), P("dp", "mp")),
        check_vma=False,
    )
```
